32 devices in a mesh: dp: 8 (over z, x), owner: 4 (over y, core).
Axes of the slice: x: 2, y: 2, z: 4, core: 2. Of those that a mesh axis runs over, the one named last changes fastest.
Arguments:
- grads: bfloat16 [8, 10, 1024, 1024], P('dp', None, None, 'owner'), may hold values from -0.059814453 to 0.059814453
- owner_of: int32 [10], replicated, may hold values from 0 to 3, as said below
- left_stats: float32 [4, 6, 1024, 1024], P('owner', None, 'dp'), may hold values from -6 to 6
- right_stats: float32 [4, 6, 1024, 1024], P('owner', None, 'dp'), may hold values from -6 to 6
- left_root: bfloat16 [4, 6, 1024, 1024], P('owner', None, 'dp'), as said below
- right_root: bfloat16 [4, 6, 1024, 1024], P('owner', None, 'dp'), as said below
- weights: bfloat16 [4, 6, 1024, 1024], P('owner', None, 'dp'), may hold values from -6 to 6
- first_moment: float32 [4, 6, 1024, 1024], P('owner', None, 'dp'), may hold values from -3 to 3
- second_moment: float32 [4, 6, 1024, 1024], P('owner', None, 'dp'), may hold values from 0.0001 to 0.01
Outputs:
- new_left: float32 [4, 6, 1024, 1024], P('owner', None, 'dp')
- new_right: float32 [4, 6, 1024, 1024], P('owner', None, 'dp')
- new_first: float32 [4, 6, 1024, 1024], P('owner', None, 'dp')
- new_second: float32 [4, 6, 1024, 1024], P('owner', None, 'dp')
- new_weights: bfloat16 [10, 1024, 1024], P(None, None, 'owner')
The draws below stay inside these ranges and needn't reach their ends.
Inputs may be any that keep to these rules, and one draw needn't show every extreme that they name: `owner_of`: no owner holds more than 6 blocks, and one owner holds exactly 6. `left_root`: Symmetric. `right_root`: Symmetric.
All inputs are finite; a program needn't handle non-finite values.
Results may differ from the reference program's by a relative error of at most 0.012.
Values may be sent and summed in bfloat16 or wider, within the bound.
A program may use at most 192 MiB of HBM per device.

```python
import math
import jax
import jax.numpy as jnp
from jax import lax

BLOCK = 1024
MATS = 10
SLOTS = 6
OWNERS = 4
REPLICAS = 8


def draw_owner_of(key, part):
    first_key, second_key, third_key = jax.random.split(jax.random.fold_in(key, 11), 3)
    order = jax.random.permutation(first_key, MATS)
    rank = jnp.argsort(order)
    busiest = jax.random.randint(second_key, (), 0, OWNERS)
    others = jax.random.randint(third_key, (MATS,), 0, OWNERS - 1)
    others = others + (others >= busiest).astype(jnp.int32)
    return jnp.where(rank < SLOTS, busiest, others).astype(jnp.int32)


def root_draw(key):
    base_key, diag_key = jax.random.split(key)
    base = jax.random.normal(base_key, (OWNERS, SLOTS, BLOCK, BLOCK), jnp.float32) * (0.5 / BLOCK ** 0.5)
    mirror = (base + jnp.swapaxes(base, -1, -2)) * 0.7071
    diagonal = jnp.exp(jax.random.uniform(diag_key, (OWNERS, SLOTS, BLOCK), jnp.float32, -0.6931, 0.6931))
    rows_at = lax.broadcasted_iota(jnp.int32, (BLOCK, BLOCK), 0)
    cols_at = lax.broadcasted_iota(jnp.int32, (BLOCK, BLOCK), 1)
    unit = (rows_at == cols_at).astype(jnp.float32)
    return (mirror + unit * diagonal[..., None]).astype(jnp.bfloat16)


def draw_left_root(key, part):
    return root_draw(jax.random.fold_in(key, 3))


def draw_right_root(key, part):
    return root_draw(jax.random.fold_in(key, 7))


def draw_first_moment(key, part):
    value_key = jax.random.fold_in(key, 5)
    shape = (OWNERS, SLOTS, BLOCK, BLOCK)
    position = lax.broadcasted_iota(jnp.float32, (BLOCK, 1), 0) / (BLOCK - 1)
    values = jax.random.normal(value_key, shape, jnp.float32) * 0.05
    row_scale = jnp.exp(position * 2.1972)
    return jnp.clip(values * row_scale, -3.0, 3.0)


def strengthened(values, rng, source, target, blocks, factor):
    def block_of(dim):
        return (jnp.arange(values.shape[dim]) // (values.shape[dim] // blocks)).reshape((-1,) + (1,) * (values.ndim - 1 - dim))

    first = jax.random.permutation(rng, blocks)[block_of(target)]
    other_side = (block_of(target) + blocks // 2) % blocks
    return jnp.where((block_of(source) == first) | (block_of(source) == other_side), factor * values, values)


def block_levels(stream_key, dims, shards, least, largest):
    factor_of = 1.0
    for dim, blocks in shards:
        heights = jax.random.uniform(jax.random.fold_in(jax.random.fold_in(stream_key, 6), dim), (blocks,), jnp.float32, least / len(shards), largest / len(shards))
        factor_of = factor_of * jnp.repeat(jnp.exp(heights), dims[dim] // blocks).reshape((-1,) + (1,) * (len(dims) - 1 - dim))
    return factor_of


def bell_draw(stream_key, shape, deviation, limit, cuts=(), kind=jnp.bfloat16):
    factor_of = block_levels(stream_key, shape, cuts, -0.22, 0.18) if cuts else 1.0
    entries = jax.random.normal(stream_key, shape, jnp.float32) * deviation * factor_of
    return jnp.minimum(jnp.maximum(entries, -limit), limit).astype(kind)


def noise_with(key, dims, deviation, bound, cuts, heavy, dtype=jnp.bfloat16):
    values = deviation * jax.random.normal(key, dims, jnp.float32)
    if cuts:
        values = values * block_levels(key, dims, cuts, -0.22, 0.18)
    return jnp.clip(strengthened(values, jax.random.fold_in(key, 3), *heavy), -bound, bound).astype(dtype)


def setup_inputs(seed: int = 0) -> dict:
    key_list = jax.random.split(jax.random.key(seed), 10)
    return {
        "grads": noise_with(key_list[0], (REPLICAS, MATS, BLOCK, BLOCK), 0.01, 0.059814453, ((0, 8), (3, 4)), (0, 2, 8, 2.0)),
        "owner_of": draw_owner_of(jax.random.fold_in(key_list[9], 71), 0),
        "left_stats": bell_draw(key_list[2], (OWNERS, SLOTS, BLOCK, BLOCK), 1.0, 6.0, ((0, 4), (2, 8)), jnp.float32),
        "right_stats": bell_draw(key_list[3], (OWNERS, SLOTS, BLOCK, BLOCK), 1.0, 6.0, ((0, 4), (2, 8)), jnp.float32),
        "left_root": draw_left_root(jax.random.fold_in(key_list[9], 71), 0),
        "right_root": draw_right_root(jax.random.fold_in(key_list[9], 71), 0),
        "weights": bell_draw(key_list[6], (OWNERS, SLOTS, BLOCK, BLOCK), 1.0, 6.0, ((0, 4), (2, 8))),
        "first_moment": draw_first_moment(jax.random.fold_in(key_list[9], 71), 0),
        "second_moment": jnp.clip(jnp.exp(math.log(0.01) - 4.6051702 * jax.random.uniform(key_list[8], (OWNERS, SLOTS, BLOCK, BLOCK), jnp.float32) ** block_levels(key_list[8], (OWNERS, SLOTS, BLOCK, BLOCK), ((0, 4), (2, 8)), -0.2, 0.2)), 0.0001, 0.01),
    }


def slot_table(owner_of):
    count = owner_of.shape[0]
    here = lax.broadcasted_iota(jnp.int32, (count, count), 0)
    prior = lax.broadcasted_iota(jnp.int32, (count, count), 1)
    same = (owner_of[:, None] == owner_of[None, :]) & (prior < here)
    return lax.optimization_barrier(jnp.sum(same.astype(jnp.int32), axis=1)).astype(jnp.int32)

def reference(grads, owner_of, left_stats, right_stats, left_root, right_root, weights, first_moment, second_moment):

    def accumulate(total, part):
        return (total + part.astype(jnp.float32), None)
    summed, _ = lax.scan(accumulate, jnp.zeros((MATS, BLOCK, BLOCK), jnp.float32), grads)
    slot_of = slot_table(owner_of)
    targets = (owner_of * SLOTS + slot_of).astype(jnp.int32)

    def flat(array):
        return array.reshape((OWNERS * SLOTS, BLOCK, BLOCK))

    def update_slot(inputs):
        index, left, right, lroot, rroot, weight, first, second = inputs
        pick = (targets == index).astype(jnp.float32)
        grad = jnp.einsum('m,mij->ij', pick, summed, precision=lax.Precision.HIGHEST)
        rounded = grad.astype(jnp.bfloat16)
        new_left = 0.95 * left + jnp.dot(rounded, rounded.T, preferred_element_type=jnp.float32)
        new_right = 0.95 * right + jnp.dot(rounded.T, rounded, preferred_element_type=jnp.float32)
        half = jnp.dot(lroot, rounded, preferred_element_type=jnp.float32).astype(jnp.bfloat16)
        direction = jnp.dot(half, rroot, preferred_element_type=jnp.float32)
        new_first = 0.9 * first + 0.1 * grad
        new_second = 0.999 * second + 0.001 * grad * grad
        adam = new_first / (jnp.sqrt(new_second) + 1e-08)
        graft = jnp.sqrt(jnp.sum(adam * adam)) / jnp.sqrt(jnp.sum(direction * direction) + 1e-12)
        moved = weight.astype(jnp.float32) - 0.1 * graft * direction
        updated = moved * lax.rsqrt(lax.optimization_barrier(jnp.mean(moved * moved, axis=-1, keepdims=True)) + 1e-06)
        return (new_left, new_right, new_first, new_second, updated)
    indices = jnp.arange(OWNERS * SLOTS).astype(jnp.int32)
    new_left, new_right, new_first, new_second, updated = lax.map(update_slot, (indices, flat(left_stats), flat(right_stats), flat(left_root), flat(right_root), flat(weights), flat(first_moment), flat(second_moment)))
    new_weights = jnp.take(updated, targets, axis=0).astype(jnp.bfloat16)
    shape = (OWNERS, SLOTS, BLOCK, BLOCK)
    return (new_left.reshape(shape), new_right.reshape(shape), new_first.reshape(shape), new_second.reshape(shape), new_weights)
```

```python
import jax
import jax.numpy as jnp
from jax import lax
from jax.sharding import Mesh, PartitionSpec as P

CORES = 2
GRID = ("y", "core")


def slot_table(owner_of):
    count = owner_of.shape[0]
    here = lax.broadcasted_iota(jnp.int32, (count, count), 0)
    prior = lax.broadcasted_iota(jnp.int32, (count, count), 1)
    same = (owner_of[:, None] == owner_of[None, :]) & (prior < here)
    return jnp.sum(same.astype(jnp.int32), axis=1)


def sum_rows(grads):
    return lax.psum_scatter(grads, "dp", scatter_dimension=1, tiled=True)


def gather_rows(part):
    return lax.all_gather(part, ("dp", "core"), axis=1, tiled=True)


def dot(a, b, dims):
    return lax.dot_general(a, b, (dims, ((0,), (0,))), preferred_element_type=jnp.float32)


def per_device(
    grads,
    owner_of,
    left_stats,
    right_stats,
    left_root,
    right_root,
    weights,
    first_moment,
    second_moment,
):
    planes = lax.axis_size("y")
    y = lax.axis_index("y")
    core = lax.axis_index("core")
    me = y * CORES + core
    slots, rows, width = left_stats.shape[1:]
    count = owner_of.shape[0]
    per_plane = -(-count // planes)
    padded = per_plane * planes
    part = rows // CORES
    slot_of = slot_table(owner_of)

    mine = owner_of == me
    slot_at = lax.broadcasted_iota(jnp.int32, (slots, count), 0)
    holds = mine[None, :] & (slot_of[None, :] == slot_at)
    has = jnp.any(holds, axis=1)
    block_of = jnp.argmax(holds, axis=1).astype(jnp.int32)

    def by_block(array):
        picked = jnp.where(mine[:, None, None], jnp.take(array[0], slot_of, axis=0), 0)
        return jnp.pad(picked, ((0, padded - count), (0, 0), (0, 0)))

    def to_plane(arrays):
        picked = jnp.stack([by_block(array) for array in arrays])
        kinds = len(arrays)
        picked = picked.reshape(kinds, planes, per_plane, CORES, part, width)
        picked = picked.transpose(1, 3, 0, 2, 4, 5).reshape(-1, kinds * per_plane, part, width)
        out = lax.psum_scatter(picked, GRID, scatter_dimension=0, tiled=True)
        return out.reshape(kinds, per_plane, part, width)

    rroot, lroot, weight = to_plane((right_root, left_root, weights))
    rroot_all = gather_rows(rroot)

    reduced = sum_rows(grads[0])
    summed = lax.all_gather(reduced, GRID, axis=2, tiled=True)
    wide = jnp.pad(summed, ((0, padded - count), (0, 0), (0, 0)))
    own = lax.dynamic_slice(wide, (y * per_plane, core * part, 0), (per_plane, part, width))
    full = gather_rows(own)

    first_row = lax.axis_index("dp") * rows + core * part
    own_cols = lax.dynamic_slice_in_dim(full, first_row, part, 2)
    half = dot(lroot, full, ((2,), (1,))).astype(jnp.bfloat16)
    left_inc = dot(own, full, ((2,), (2,))).astype(jnp.bfloat16)
    right_inc = dot(own_cols, full, ((1,), (1,))).astype(jnp.bfloat16)
    incs = lax.all_gather(jnp.stack([left_inc, right_inc]), GRID)
    incs = incs.reshape(planes, CORES, 2, per_plane, part, width)
    incs = incs.transpose(2, 0, 3, 1, 4, 5).reshape(2, padded, rows, width)

    def to_slots(array):
        return jnp.where(has[:, None, None], jnp.take(array, block_of, axis=0), 0).astype(jnp.float32)

    owned = to_slots(summed)
    new_left = 0.95 * left_stats[0] + to_slots(incs[0])
    new_right = 0.95 * right_stats[0] + to_slots(incs[1])
    new_first = 0.9 * first_moment[0] + 0.1 * owned
    new_second = 0.999 * second_moment[0] + 0.001 * owned * owned
    adam = new_first / (jnp.sqrt(new_second) + 1e-08)
    adam_sq = jnp.sum(adam * adam, axis=(1, 2))
    adam_part = jnp.sum(jnp.where(holds, adam_sq[:, None], 0.0), axis=0)

    direction = dot(half, rroot_all, ((2,), (1,)))
    dir_sq = jnp.sum(direction * direction, axis=(1, 2))
    dir_part = lax.dynamic_update_slice(jnp.zeros((padded,), jnp.float32), dir_sq, (y * per_plane,))
    totals = lax.psum(
        jnp.concatenate([jnp.pad(adam_part, (0, padded - count)), dir_part]), ("dp",) + GRID
    )
    graft = jnp.sqrt(totals[:padded]) / jnp.sqrt(totals[padded:] + 1e-12)
    graft = lax.dynamic_slice(graft, (y * per_plane,), (per_plane,))
    moved = weight.astype(jnp.float32) - 0.1 * graft[:, None, None] * direction
    updated = moved * lax.rsqrt(jnp.mean(moved * moved, axis=-1, keepdims=True) + 1e-06)
    finished = updated.astype(jnp.bfloat16).reshape(per_plane, part, planes * CORES, -1)
    by_cols = lax.all_to_all(finished, GRID, split_axis=2, concat_axis=0, tiled=False)
    by_cols = by_cols.reshape(planes, CORES, per_plane, part, -1)
    by_cols = by_cols.transpose(0, 2, 1, 3, 4).reshape(padded, rows, -1)[:count]
    new_weights = lax.all_gather(by_cols, "dp", axis=1, tiled=True)
    return (new_left[None], new_right[None], new_first[None], new_second[None], new_weights)


def solution(mesh):
    dp, owners = mesh.shape["dp"], mesh.shape["owner"]
    grid = Mesh(mesh.devices.reshape(dp, owners // CORES, CORES), ("dp",) + GRID)
    rows = P(GRID, None, "dp", None)
    return jax.shard_map(
        per_device,
        mesh=grid,
        in_specs=(P("dp", None, None, GRID), P()) + (rows,) * 7,
        out_specs=(rows,) * 4 + (P(None, None, GRID),),
        check_vma=False,
    )
```

```python
import functools

import jax
import jax.numpy as jnp
from jax import lax
from jax.experimental import pallas as pl
from jax.experimental.pallas import tpu as pltpu
from jax.sharding import Mesh, PartitionSpec as P

MESH = pl.DeviceIdType.MESH

CORES = 2
GRID = ("y", "core")


def slot_table(owner_of):
    count = owner_of.shape[0]
    here = lax.broadcasted_iota(jnp.int32, (count, count), 0)
    prior = lax.broadcasted_iota(jnp.int32, (count, count), 1)
    same = (owner_of[:, None] == owner_of[None, :]) & (prior < here)
    return jnp.sum(same.astype(jnp.int32), axis=1)


def grid_of(n):
    width = 1
    while 2 * (2 * width) ** 2 <= n:
        width *= 2
    return n // width, width


def position_of(index, n):
    depth, width = grid_of(n)
    z, x = index // width, index % width
    row = depth - 1 - z
    odd = row % 2
    along = (1 - odd) * (x - 1) + odd * (width - 1 - x)
    back = (x + width - 1) // width
    return (1 - back) * z + back * (depth + row * (width - 1) + along)


def index_at(position, n):
    depth, width = grid_of(n)
    back = (position // depth + width - 1) // width
    rest = position - depth + (1 - back) * n
    row, along = rest // (width - 1), rest % (width - 1)
    odd = row % 2
    x = (1 - odd) * (1 + along) + odd * (width - 1 - along)
    return (1 - back) * position * width + back * ((depth - 1 - row) * width + x)


def ring(n):
    way = 1 - 2 * lax.axis_index("core")
    place = position_of(lax.axis_index("dp"), n)
    return place, way, index_at((place + way + n) % n, n), index_at((place - way + n) % n, n)


def sum_kernel(n, rows, g_ref, out_ref, held, send_sem, recv_sem):
    place, way, after, before = ring(n)
    half = g_ref.shape[0] // 2
    barrier = pltpu.get_barrier_semaphore()
    pl.semaphore_signal(barrier, inc=1, device_id={"dp": before}, device_id_type=MESH)
    pl.semaphore_wait(barrier, 1)

    def terms(step, part):
        row = index_at((place - way * (1 + step) + 2 * n) % n, n) * rows
        return g_ref.at[pl.ds(part * half, half), pl.ds(pl.multiple_of(row, rows), rows), :]

    def send(source, step, part):
        return pltpu.make_async_remote_copy(
            src_ref=source,
            dst_ref=held.at[step, part],
            send_sem=send_sem.at[step, part],
            recv_sem=recv_sem.at[step, part],
            device_id={"dp": after},
            device_id_type=MESH,
        )

    def total(step, part):
        came = held[step - 1, part].astype(jnp.float32)
        return (came + terms(step, part)[...].astype(jnp.float32)).astype(jnp.bfloat16)

    for part in range(2):
        send(terms(0, part), 0, part).start()

    @pl.loop(1, n - 1)
    def _(step):
        for part in range(2):
            send(held.at[step - 1, part], step - 1, part).wait_recv()
            held[step - 1, part] = total(step, part)
            send(held.at[step - 1, part], step, part).start()

    for part in range(2):
        send(held.at[n - 2, part], n - 2, part).wait_recv()
        out_ref[pl.ds(part * half, half)] = total(n - 1, part)

    @pl.loop(0, n - 1)
    def _(step):
        for part in range(2):
            send(held.at[step, part], step, part).wait_send()


def sum_rows(grads):
    n = lax.axis_size("dp")
    count, height, width = grads.shape
    rows = height // n
    return pl.pallas_call(
        functools.partial(sum_kernel, n, rows),
        out_shape=jax.ShapeDtypeStruct((count, rows, width), grads.dtype),
        in_specs=[pl.BlockSpec(memory_space=pltpu.VMEM)],
        out_specs=pl.BlockSpec(memory_space=pltpu.VMEM),
        scratch_shapes=[
            pltpu.VMEM((n - 1, 2, count // 2, rows, width), grads.dtype),
            pltpu.SemaphoreType.DMA((n - 1, 2)),
            pltpu.SemaphoreType.DMA((n - 1, 2)),
        ],
        compiler_params=pltpu.CompilerParams(
            collective_id=0, has_side_effects=True, vmem_limit_bytes=24 * 2**20
        ),
        cost_estimate=pl.CostEstimate(flops=0, bytes_accessed=200_000_000, transcendentals=0),
        name="sum_ring",
    )(grads)


def gather_kernel(n, shared, x_ref, out_ref, local_sem, send_sem, recv_sem, *pair_sems):
    place, way, after, before = ring(n)
    rows = x_ref.shape[1]
    core = lax.axis_index("core")
    other = {"core": 1 - core}
    barrier = pltpu.get_barrier_semaphore()
    pl.semaphore_signal(barrier, inc=1, device_id={"dp": before}, device_id_type=MESH)
    if shared:
        pl.semaphore_signal(barrier, inc=1, device_id=other, device_id_type=MESH)
    pl.semaphore_wait(barrier, 2 if shared else 1)

    def spot(step):
        index = index_at((place - way * step + 2 * n) % n, n)
        first = (index * CORES + core) * rows if shared else index * rows
        return out_ref.at[:, pl.ds(pl.multiple_of(first, rows), rows), :]

    def copy(step, sems, target):
        return pltpu.make_async_remote_copy(
            src_ref=spot(step),
            dst_ref=spot(step),
            send_sem=sems[0].at[step],
            recv_sem=sems[1].at[step],
            device_id=target,
            device_id_type=MESH,
        )

    def onward(step):
        return copy(step, (send_sem, recv_sem), {"dp": after})

    own = pltpu.make_async_copy(x_ref, spot(0), local_sem)
    own.start()
    own.wait()
    onward(0).start()
    if shared:
        copy(0, pair_sems, other).start()

    @pl.loop(1, n)
    def _(step):
        onward(step - 1).wait_recv()

        @pl.when(step < n - 1)
        def _():
            onward(step).start()

        if shared:
            copy(step, pair_sems, other).start()

    @pl.loop(0, n)
    def _(step):
        @pl.when(step < n - 1)
        def _():
            onward(step).wait_send()

        if shared:
            copy(step, pair_sems, other).wait()


def gather_ring(part, shared, number):
    n = lax.axis_size("dp")
    count, rows, width = part.shape
    height = n * rows * (CORES if shared else 1)
    return pl.pallas_call(
        functools.partial(gather_kernel, n, shared),
        out_shape=jax.ShapeDtypeStruct((count, height, width), part.dtype),
        in_specs=[pl.BlockSpec(memory_space=pl.ANY)],
        out_specs=pl.BlockSpec(memory_space=pl.ANY),
        scratch_shapes=[pltpu.SemaphoreType.DMA]
        + [pltpu.SemaphoreType.DMA((n - 1,))] * 2
        + ([pltpu.SemaphoreType.DMA((n,))] * 2 if shared else []),
        compiler_params=pltpu.CompilerParams(collective_id=number, has_side_effects=True),
        cost_estimate=pl.CostEstimate(flops=0, bytes_accessed=200_000_000, transcendentals=0),
        name="gather_ring_%d" % number,
    )(part)


def gather_rows(part):
    return lax.all_gather(part, ("dp", "core"), axis=1, tiled=True)


def dot(a, b, dims):
    return lax.dot_general(a, b, (dims, ((0,), (0,))), preferred_element_type=jnp.float32)


def per_device(
    grads,
    owner_of,
    left_stats,
    right_stats,
    left_root,
    right_root,
    weights,
    first_moment,
    second_moment,
):
    planes = lax.axis_size("y")
    y = lax.axis_index("y")
    core = lax.axis_index("core")
    me = y * CORES + core
    slots, rows, width = left_stats.shape[1:]
    count = owner_of.shape[0]
    per_plane = -(-count // planes)
    padded = per_plane * planes
    part = rows // CORES
    slot_of = slot_table(owner_of)

    mine = owner_of == me
    slot_at = lax.broadcasted_iota(jnp.int32, (slots, count), 0)
    holds = mine[None, :] & (slot_of[None, :] == slot_at)
    has = jnp.any(holds, axis=1)
    block_of = jnp.argmax(holds, axis=1).astype(jnp.int32)

    def by_block(array):
        picked = jnp.stack([
            jnp.where(mine[m], lax.dynamic_index_in_dim(array[0], slot_of[m], 0, False), 0)
            for m in range(count)
        ])
        return jnp.pad(picked, ((0, padded - count), (0, 0), (0, 0)))

    def to_plane(arrays):
        picked = jnp.stack([by_block(array) for array in arrays])
        kinds = len(arrays)
        picked = picked.reshape(kinds, planes, per_plane, CORES, part, width)
        picked = picked.transpose(1, 3, 0, 2, 4, 5).reshape(-1, kinds * per_plane, part, width)
        out = lax.psum_scatter(picked, GRID, scatter_dimension=0, tiled=True)
        return out.reshape(kinds, per_plane, part, width)

    rroot, lroot, weight = to_plane((right_root, left_root, weights))
    rroot_all = gather_rows(rroot)

    reduced = sum_rows(grads[0])
    summed = lax.all_gather(reduced, GRID, axis=2, tiled=True)
    wide = jnp.pad(summed, ((0, padded - count), (0, 0), (0, 0)))
    own = lax.dynamic_slice(wide, (y * per_plane, core * part, 0), (per_plane, part, width))
    full = gather_ring(own, True, 1)

    first_row = lax.axis_index("dp") * rows + core * part
    own_cols = lax.dynamic_slice_in_dim(full, first_row, part, 2)
    half = dot(lroot, full, ((2,), (1,))).astype(jnp.bfloat16)
    left_inc = dot(own, full, ((2,), (2,))).astype(jnp.bfloat16)
    right_inc = dot(own_cols, full, ((1,), (1,))).astype(jnp.bfloat16)
    incs = lax.all_gather(jnp.stack([left_inc, right_inc]), GRID)
    incs = incs.reshape(planes, CORES, 2, per_plane, part, width)
    incs = incs.transpose(2, 0, 3, 1, 4, 5).reshape(2, padded, rows, width)

    def to_slots(array):
        return jnp.stack([
            jnp.where(has[k], lax.dynamic_index_in_dim(array, block_of[k], 0, False), 0)
            for k in range(slots)
        ]).astype(jnp.float32)

    owned = to_slots(summed)
    new_left = 0.95 * left_stats[0] + to_slots(incs[0])
    new_right = 0.95 * right_stats[0] + to_slots(incs[1])
    new_first = 0.9 * first_moment[0] + 0.1 * owned
    new_second = 0.999 * second_moment[0] + 0.001 * owned * owned
    adam = new_first / (jnp.sqrt(new_second) + 1e-08)
    adam_sq = jnp.sum(adam * adam, axis=(1, 2))
    adam_part = jnp.sum(jnp.where(holds, adam_sq[:, None], 0.0), axis=0)

    direction = dot(half, rroot_all, ((2,), (1,)))
    dir_sq = jnp.sum(direction * direction, axis=(1, 2))
    dir_part = lax.dynamic_update_slice(jnp.zeros((padded,), jnp.float32), dir_sq, (y * per_plane,))
    totals = lax.psum(
        jnp.concatenate([jnp.pad(adam_part, (0, padded - count)), dir_part]), ("dp",) + GRID
    )
    graft = jnp.sqrt(totals[:padded]) / jnp.sqrt(totals[padded:] + 1e-12)
    graft = lax.dynamic_slice(graft, (y * per_plane,), (per_plane,))
    moved = weight.astype(jnp.float32) - 0.1 * graft[:, None, None] * direction
    updated = moved * lax.rsqrt(jnp.mean(moved * moved, axis=-1, keepdims=True) + 1e-06)
    finished = updated.astype(jnp.bfloat16).reshape(per_plane, part, planes * CORES, -1)
    by_cols = lax.all_to_all(finished, GRID, split_axis=2, concat_axis=0, tiled=False)
    by_cols = by_cols.reshape(planes, CORES, per_plane, part, -1)
    by_cols = by_cols.transpose(0, 2, 1, 3, 4).reshape(padded, rows, -1)[:count]
    new_weights = gather_ring(by_cols, False, 2)
    return (new_left[None], new_right[None], new_first[None], new_second[None], new_weights)


def solution(mesh):
    dp, owners = mesh.shape["dp"], mesh.shape["owner"]
    grid = Mesh(mesh.devices.reshape(dp, owners // CORES, CORES), ("dp",) + GRID)
    rows = P(GRID, None, "dp", None)
    return jax.shard_map(
        per_device,
        mesh=grid,
        in_specs=(P("dp", None, None, GRID), P()) + (rows,) * 7,
        out_specs=(rows,) * 4 + (P(None, None, GRID),),
        check_vma=False,
    )
```

```python
import functools

import jax
import jax.numpy as jnp
from jax import lax
from jax.experimental import pallas as pl
from jax.experimental.pallas import tpu as pltpu
from jax.sharding import Mesh, PartitionSpec as P

MESH = pl.DeviceIdType.MESH

CORES = 2
GRID = ("y", "core")


def slot_table(owner_of):
    count = owner_of.shape[0]
    here = lax.broadcasted_iota(jnp.int32, (count, count), 0)
    prior = lax.broadcasted_iota(jnp.int32, (count, count), 1)
    same = (owner_of[:, None] == owner_of[None, :]) & (prior < here)
    return jnp.sum(same.astype(jnp.int32), axis=1)


def grid_of(n):
    width = 1
    while 2 * (2 * width) ** 2 <= n:
        width *= 2
    return n // width, width


def position_of(index, n):
    depth, width = grid_of(n)
    z, x = index // width, index % width
    row = depth - 1 - z
    odd = row % 2
    along = (1 - odd) * (x - 1) + odd * (width - 1 - x)
    back = (x + width - 1) // width
    return (1 - back) * z + back * (depth + row * (width - 1) + along)


def index_at(position, n):
    depth, width = grid_of(n)
    back = (position // depth + width - 1) // width
    rest = position - depth + (1 - back) * n
    row, along = rest // (width - 1), rest % (width - 1)
    odd = row % 2
    x = (1 - odd) * (1 + along) + odd * (width - 1 - along)
    return (1 - back) * position * width + back * ((depth - 1 - row) * width + x)


def ring(n):
    way = 1 - 2 * lax.axis_index("core")
    place = position_of(lax.axis_index("dp"), n)
    return place, way, index_at((place + way + n) % n, n), index_at((place - way + n) % n, n)


def sum_kernel(n, rows, g_ref, out_ref, held, send_sem, recv_sem):
    place, way, after, before = ring(n)
    half = g_ref.shape[0] // 2
    barrier = pltpu.get_barrier_semaphore()
    pl.semaphore_signal(barrier, inc=1, device_id={"dp": before}, device_id_type=MESH)
    pl.semaphore_wait(barrier, 1)

    def terms(step, part):
        row = index_at((place - way * (1 + step) + 2 * n) % n, n) * rows
        return g_ref.at[pl.ds(part * half, half), pl.ds(pl.multiple_of(row, rows), rows), :]

    def send(source, step, part):
        return pltpu.make_async_remote_copy(
            src_ref=source,
            dst_ref=held.at[step, part],
            send_sem=send_sem.at[step, part],
            recv_sem=recv_sem.at[step, part],
            device_id={"dp": after},
            device_id_type=MESH,
        )

    def total(step, part):
        came = held[step - 1, part].astype(jnp.float32)
        return (came + terms(step, part)[...].astype(jnp.float32)).astype(jnp.bfloat16)

    for part in range(2):
        send(terms(0, part), 0, part).start()

    @pl.loop(1, n - 1)
    def _(step):
        for part in range(2):
            send(held.at[step - 1, part], step - 1, part).wait_recv()
            held[step - 1, part] = total(step, part)
            send(held.at[step - 1, part], step, part).start()

    for part in range(2):
        send(held.at[n - 2, part], n - 2, part).wait_recv()
        out_ref[pl.ds(part * half, half)] = total(n - 1, part)

    @pl.loop(0, n - 1)
    def _(step):
        for part in range(2):
            send(held.at[step, part], step, part).wait_send()


def sum_rows(grads):
    n = lax.axis_size("dp")
    count, height, width = grads.shape
    rows = height // n
    return pl.pallas_call(
        functools.partial(sum_kernel, n, rows),
        out_shape=jax.ShapeDtypeStruct((count, rows, width), grads.dtype),
        in_specs=[pl.BlockSpec(memory_space=pltpu.VMEM)],
        out_specs=pl.BlockSpec(memory_space=pltpu.VMEM),
        scratch_shapes=[
            pltpu.VMEM((n - 1, 2, count // 2, rows, width), grads.dtype),
            pltpu.SemaphoreType.DMA((n - 1, 2)),
            pltpu.SemaphoreType.DMA((n - 1, 2)),
        ],
        compiler_params=pltpu.CompilerParams(
            collective_id=0, has_side_effects=True, vmem_limit_bytes=24 * 2**20
        ),
        cost_estimate=pl.CostEstimate(flops=0, bytes_accessed=200_000_000, transcendentals=0),
        name="sum_ring",
    )(grads)


def gather_kernel(n, shared, x_ref, out_ref, send_sem, recv_sem, *pair_sems):
    place, way, after, before = ring(n)
    count, rows = x_ref.shape[:2]
    half = count // 2
    core = lax.axis_index("core")
    other = {"core": 1 - core}
    barrier = pltpu.get_barrier_semaphore()
    pl.semaphore_signal(barrier, inc=1, device_id={"dp": before}, device_id_type=MESH)
    if shared:
        pl.semaphore_signal(barrier, inc=1, device_id=other, device_id_type=MESH)
    pl.semaphore_wait(barrier, 2 if shared else 1)

    def first_row(step):
        index = index_at((place - way * step + 2 * n) % n, n)
        first = (index * CORES + core) * rows if shared else index * rows
        return pl.multiple_of(first, rows)

    def copy(step, part, sems, target):
        blocks = pl.ds(part * half, half if part == 0 else count - half)
        spot = out_ref.at[blocks, pl.ds(first_row(step), rows), :]
        return pltpu.make_async_remote_copy(
            src_ref=spot,
            dst_ref=spot,
            send_sem=sems[0].at[step, part],
            recv_sem=sems[1].at[step, part],
            device_id=target,
            device_id_type=MESH,
        )

    def onward(step, part):
        return copy(step, part, (send_sem, recv_sem), {"dp": after})

    out_ref[:, pl.ds(first_row(0), rows), :] = x_ref[...]
    for part in range(2):
        onward(0, part).start()
        if shared:
            copy(0, part, pair_sems, other).start()

    @pl.loop(1, n)
    def _(step):
        for part in range(2):
            onward(step - 1, part).wait_recv()

            @pl.when(step < n - 1)
            def _():
                onward(step, part).start()

            if shared:
                copy(step, part, pair_sems, other).start()

    @pl.loop(0, n)
    def _(step):
        for part in range(2):

            @pl.when(step < n - 1)
            def _():
                onward(step, part).wait_send()

            if shared:
                copy(step, part, pair_sems, other).wait()


def gather_ring(part, shared, number):
    n = lax.axis_size("dp")
    count, rows, width = part.shape
    height = n * rows * (CORES if shared else 1)
    return pl.pallas_call(
        functools.partial(gather_kernel, n, shared),
        out_shape=jax.ShapeDtypeStruct((count, height, width), part.dtype),
        in_specs=[pl.BlockSpec(memory_space=pltpu.VMEM)],
        out_specs=pl.BlockSpec(memory_space=pltpu.VMEM),
        scratch_shapes=[pltpu.SemaphoreType.DMA((n - 1, 2))] * 2
        + ([pltpu.SemaphoreType.DMA((n, 2))] * 2 if shared else []),
        compiler_params=pltpu.CompilerParams(
            collective_id=number, has_side_effects=True, vmem_limit_bytes=24 * 2**20
        ),
        cost_estimate=pl.CostEstimate(flops=0, bytes_accessed=200_000_000, transcendentals=0),
        name="gather_ring_%d" % number,
    )(part)


def dot(a, b, dims):
    return lax.dot_general(a, b, (dims, ((0,), (0,))), preferred_element_type=jnp.float32)


def per_device(
    grads,
    owner_of,
    left_stats,
    right_stats,
    left_root,
    right_root,
    weights,
    first_moment,
    second_moment,
):
    planes = lax.axis_size("y")
    y = lax.axis_index("y")
    core = lax.axis_index("core")
    me = y * CORES + core
    slots, rows, width = left_stats.shape[1:]
    count = owner_of.shape[0]
    per_plane = -(-count // planes)
    padded = per_plane * planes
    part = rows // CORES
    slot_of = slot_table(owner_of)

    mine = owner_of == me
    slot_at = lax.broadcasted_iota(jnp.int32, (slots, count), 0)
    holds = mine[None, :] & (slot_of[None, :] == slot_at)
    has = jnp.any(holds, axis=1)
    block_of = jnp.argmax(holds, axis=1).astype(jnp.int32)

    def by_block(array):
        picked = jnp.stack([
            jnp.where(mine[m], lax.dynamic_index_in_dim(array[0], slot_of[m], 0, False), 0)
            for m in range(count)
        ])
        return jnp.pad(picked, ((0, padded - count), (0, 0), (0, 0)))

    def to_send(arrays):
        picked = jnp.stack([by_block(array) for array in arrays])
        kinds = len(arrays)
        picked = picked.reshape(kinds, planes, per_plane, CORES, part, width)
        return picked.transpose(1, 3, 0, 2, 4, 5).reshape(-1, kinds * per_plane, part, width)

    picked, terms = lax.optimization_barrier((to_send((right_root, left_root, weights)), grads[0]))
    placed = lax.psum_scatter(picked, GRID, scatter_dimension=0, tiled=True)

    reduced, placed = lax.optimization_barrier((sum_rows(terms), placed))
    rroot, lroot, weight = placed.reshape(-1, per_plane, part, width)
    summed = lax.all_gather(reduced, GRID, axis=2, tiled=True)
    wide = jnp.pad(summed, ((0, padded - count), (0, 0), (0, 0)))
    own = lax.dynamic_slice(wide, (y * per_plane, core * part, 0), (per_plane, part, width))
    full = gather_ring(own, True, 1)

    first_row = lax.axis_index("dp") * rows + core * part
    own_cols = lax.dynamic_slice_in_dim(full, first_row, part, 2)
    half = dot(lroot, full, ((2,), (1,))).astype(jnp.bfloat16)
    left_inc = dot(own, full, ((2,), (2,))).astype(jnp.bfloat16)
    right_inc = dot(own_cols, full, ((1,), (1,))).astype(jnp.bfloat16)
    incs, rroot = lax.optimization_barrier((jnp.stack([left_inc, right_inc]), rroot))
    rroot_all = gather_ring(rroot, True, 3)
    incs = lax.all_gather(incs, GRID)
    incs = incs.reshape(planes, CORES, 2, per_plane, part, width)
    incs = incs.transpose(2, 0, 3, 1, 4, 5).reshape(2, padded, rows, width)

    def to_slots(array):
        return jnp.stack([
            jnp.where(has[k], lax.dynamic_index_in_dim(array, block_of[k], 0, False), 0)
            for k in range(slots)
        ]).astype(jnp.float32)

    owned = to_slots(summed)
    new_left = 0.95 * left_stats[0] + to_slots(incs[0])
    new_right = 0.95 * right_stats[0] + to_slots(incs[1])
    new_first = 0.9 * first_moment[0] + 0.1 * owned
    new_second = 0.999 * second_moment[0] + 0.001 * owned * owned
    adam = new_first / (jnp.sqrt(new_second) + 1e-08)
    adam_sq = jnp.sum(adam * adam, axis=(1, 2))
    adam_part = jnp.sum(jnp.where(holds, adam_sq[:, None], 0.0), axis=0)

    direction = dot(half, rroot_all, ((2,), (1,)))
    dir_sq = jnp.sum(direction * direction, axis=(1, 2))
    dir_part = lax.dynamic_update_slice(jnp.zeros((padded,), jnp.float32), dir_sq, (y * per_plane,))
    totals = lax.psum(
        jnp.concatenate([jnp.pad(adam_part, (0, padded - count)), dir_part]), ("dp",) + GRID
    )
    graft = jnp.sqrt(totals[:padded]) / jnp.sqrt(totals[padded:] + 1e-12)
    graft = lax.dynamic_slice(graft, (y * per_plane,), (per_plane,))
    moved = weight.astype(jnp.float32) - 0.1 * graft[:, None, None] * direction
    updated = moved * lax.rsqrt(jnp.mean(moved * moved, axis=-1, keepdims=True) + 1e-06)
    finished = updated.astype(jnp.bfloat16).reshape(per_plane, part, planes * CORES, -1)
    by_cols = lax.all_to_all(finished, GRID, split_axis=2, concat_axis=0, tiled=False)
    by_cols = by_cols.reshape(planes, CORES, per_plane, part, -1)
    by_cols = by_cols.transpose(0, 2, 1, 3, 4).reshape(padded, rows, -1)[:count]
    new_weights = gather_ring(by_cols, False, 2)
    return (new_left[None], new_right[None], new_first[None], new_second[None], new_weights)


def solution(mesh):
    dp, owners = mesh.shape["dp"], mesh.shape["owner"]
    grid = Mesh(mesh.devices.reshape(dp, owners // CORES, CORES), ("dp",) + GRID)
    rows = P(GRID, None, "dp", None)
    return jax.shard_map(
        per_device,
        mesh=grid,
        in_specs=(P("dp", None, None, GRID), P()) + (rows,) * 7,
        out_specs=(rows,) * 4 + (P(None, None, GRID),),
        check_vma=False,
    )
```
